32 devices in a mesh: box: 4 (over z), slab: 8 (over y, x, core).
Axes of the slice: x: 2, y: 2, z: 4, core: 2. Of those that a mesh axis runs over, the one named last changes fastest.
Arguments:
- hidden_field: bfloat16 [4, 8, 64, 128, 128], P('box', None, 'slab'), may hold values from -6 to 6
- cone_grad: float32 [256, 128, 128], P(('box', 'slab')), may hold values from -6 to 6
- conv_weight: bfloat16 [8, 27], replicated, may hold values from -0.4375 to 0.4375
- box_lower: int32 [256], P(('box', 'slab')), may hold values from 0 to 3, as said below
- box_upper: int32 [256], P(('box', 'slab')), may hold values from 0 to 3, as said below
- plane_lower: int32 [256], P(('box', 'slab')), may hold values from 0 to 63, as said below
- plane_upper: int32 [256], P(('box', 'slab')), may hold values from 0 to 63, as said below
- weight_lower: int32 [256], P(('box', 'slab')), may hold values from 0 to 256
- weight_upper: int32 [256], P(('box', 'slab')), may hold values from 0 to 256, as said below
Outputs:
- hidden_grad: bfloat16 [4, 8, 64, 128, 128], P('box', None, 'slab')
- weight_grad: float32 [8, 27], replicated
The draws below stay inside these ranges and needn't reach their ends.
Inputs may be any that keep to these rules, and one draw needn't show every extreme that they name: With g = l // 64 the group of plane l, box_lower[l] is g or g - 1 (never below 0). box_upper[l] = min(box_lower[l] + 1, 3). Each box b has one offset o_b, and for one box, drawn from the seed, o_b = 32; plane_lower[l] = (l + o_b) mod 64 with b = box_lower[l]. plane_upper[l] = (l + o_b) mod 64 with b = box_upper[l], the same offsets. weight_upper[l] = 256 - weight_lower[l].
All inputs are finite; a program needn't handle non-finite values.
Results may differ from the reference program's by a relative error of at most 0.005.
Values may be sent and summed in bfloat16 or wider, within the bound.
A program may use at most 320 MiB of HBM per device.

```python
import jax
import jax.numpy as jnp
from jax import lax

CH = 8
WDEN = 256
NX = 128
NY = 128
NZ = 64
NBOX = 4
NLC = 256


def routing(key):
    base = jax.random.fold_in(key, 11)
    keys = jax.random.split(base, 4)
    offsets = jax.random.randint(keys[0], (NBOX,), 0, NZ).astype(jnp.int32)
    chosen = jax.random.randint(keys[3], (), 0, NBOX).astype(jnp.int32)
    offsets = jnp.where(jnp.arange(NBOX, dtype=jnp.int32) == chosen, jnp.int32(NZ // 2), offsets)
    planes = jnp.arange(NLC, dtype=jnp.int32)
    groups = planes // NZ
    lower_box = jnp.maximum(groups - jax.random.randint(keys[1], (NLC,), 0, 2).astype(jnp.int32), 0)
    upper_box = jnp.minimum(lower_box + 1, NBOX - 1)
    lower_plane = (planes + offsets[lower_box]) % NZ
    upper_plane = (planes + offsets[upper_box]) % NZ
    lower_weight = jax.random.randint(keys[2], (NLC,), 0, WDEN + 1).astype(jnp.int32)
    return (lower_box, upper_box, lower_plane, upper_plane, lower_weight, WDEN - lower_weight)


def draw_box_lower(key, part):
    return routing(key)[0]


def draw_box_upper(key, part):
    return routing(key)[1]


def draw_plane_lower(key, part):
    return routing(key)[2]


def draw_plane_upper(key, part):
    return routing(key)[3]


def draw_weight_lower(key, part):
    return routing(key)[4]


def draw_weight_upper(key, part):
    return routing(key)[5]


def levels(stream_key, extent, pieces, smallest, top_value):
    level = 1.0
    for axis_at, blocks in pieces:
        heights = jax.random.uniform(jax.random.fold_in(jax.random.fold_in(stream_key, 6), axis_at), (blocks,), jnp.float32, smallest / len(pieces), top_value / len(pieces))
        level = level * jnp.repeat(jnp.exp(heights), extent[axis_at] // blocks).reshape((-1,) + (1,) * (len(extent) - 1 - axis_at))
    return level


def normal_values(rng, dims, width, bound, cuts=(), held_as=jnp.bfloat16):
    drawn = width * jax.random.normal(rng, dims, jnp.float32)
    if cuts:
        drawn = drawn * levels(rng, dims, cuts, -0.22, 0.18)
    return jnp.clip(drawn, -bound, bound).astype(held_as)


def setup_inputs(seed: int = 0) -> dict:
    arg_keys = jax.random.split(jax.random.key(seed), 10)
    hidden_field = normal_values(arg_keys[0], (NBOX, CH, NZ, NX, NY), 1.0, 6.0, ((0, 4), (2, 8)))
    cone_grad = normal_values(arg_keys[1], (NLC, NX, NY), 1.0, 6.0, ((0, 32),), jnp.float32)
    conv_weight = normal_values(arg_keys[2], (CH, 27), (CH * 27) ** -0.5, 0.4375)
    box_lower = draw_box_lower(jax.random.fold_in(arg_keys[9], 71), 0)
    box_upper = draw_box_upper(jax.random.fold_in(arg_keys[9], 71), 0)
    plane_lower = draw_plane_lower(jax.random.fold_in(arg_keys[9], 71), 0)
    plane_upper = draw_plane_upper(jax.random.fold_in(arg_keys[9], 71), 0)
    weight_lower = draw_weight_lower(jax.random.fold_in(arg_keys[9], 71), 0)
    weight_upper = draw_weight_upper(jax.random.fold_in(arg_keys[9], 71), 0)
    return {"hidden_field": hidden_field, "cone_grad": cone_grad, "conv_weight": conv_weight, "box_lower": box_lower, "box_upper": box_upper, "plane_lower": plane_lower, "plane_upper": plane_upper, "weight_lower": weight_lower, "weight_upper": weight_upper}


def tap_list():
    result = []
    for shift_z in (-1, 0, 1):
        for shift_x in (-1, 0, 1):
            for shift_y in (-1, 0, 1):
                result.append((shift_z, shift_x, shift_y))
    return result

def reference(hidden_field, cone_grad, conv_weight, box_lower, box_upper, plane_lower, plane_upper, weight_lower, weight_upper):
    lower = weight_lower.astype(jnp.float32) / WDEN
    upper = weight_upper.astype(jnp.float32) / WDEN
    first = jax.ops.segment_sum(lower[:, None, None] * cone_grad, (box_lower * NZ + plane_lower).astype(jnp.int32), num_segments=NBOX * NZ)
    second = jax.ops.segment_sum(upper[:, None, None] * cone_grad, (box_upper * NZ + plane_upper).astype(jnp.int32), num_segments=NBOX * NZ)
    field_grad = (first + second).reshape(NBOX, NZ, NX, NY)
    field_low = field_grad.astype(jnp.bfloat16)
    weight_wide = conv_weight.astype(jnp.float32)

    def per_box(pair):
        block, field = pair
        wide = block.astype(jnp.float32)
        grads = jnp.zeros((CH, NZ, NX, NY), jnp.float32)
        columns = []
        for index, shifts in enumerate(tap_list()):
            moved = jnp.roll(field, shifts, axis=(0, 1, 2)).astype(jnp.float32)
            grads = grads + weight_wide[:, index][:, None, None, None] * moved
            columns.append(lax.optimization_barrier(jnp.sum(wide * moved[None], axis=(1, 2, 3))))
        return (grads.astype(jnp.bfloat16), jnp.stack(columns, 1))
    hidden_grad, partial_value = lax.map(per_box, (hidden_field, field_low))
    weight_grad = lax.optimization_barrier(jnp.sum(partial_value, axis=0)) / jnp.sqrt(jnp.float32(NBOX * NZ * NX * NY))
    return (hidden_grad, weight_grad)
```

```python
import functools
import math

import jax
import jax.numpy as jnp
from jax import lax
from jax.experimental import pallas as pl
from jax.experimental.pallas import tpu as pltpu
from jax.sharding import PartitionSpec as P

WDEN = 256
MESH = pl.DeviceIdType.MESH
F32 = jnp.float32
BF16 = jnp.bfloat16
TAP_ROWS = 32


def kernel(
    nbox,
    nslab,
    scale,
    bl,
    bu,
    plo,
    pup,
    wl,
    wu,
    cone,
    weight,
    h_hbm,
    out_hbm,
    wg,
    hbuf,
    own,
    z_up,
    z_dn,
    from_above,
    from_below,
    send_a,
    recv_a,
    send_b,
    recv_b,
    ht,
    wmat,
    wide,
    lmat,
    part,
    obuf,
    msg,
    slab_terms,
    msg2,
    box_terms,
    hsem,
    up_s,
    up_r,
    dn_s,
    dn_r,
    a_s,
    a_r,
    b_s,
    b_r,
    c_s,
    c_r,
    d_s,
    d_r,
    osem,
):
    g = lax.axis_index("box")
    me = lax.axis_index("slab")
    depth, nx, ny = cone.shape
    rows = nx // nslab
    nz = depth * nslab
    ch = hbuf.shape[0]
    pairs = ch // 2

    h_copy = pltpu.make_async_copy(h_hbm, hbuf, hsem)
    h_copy.start()

    barrier = pltpu.get_barrier_semaphore()

    def greet_slab(j, _):
        pl.semaphore_signal(barrier, inc=1, device_id={"slab": lax.rem(me + j, nslab)}, device_id_type=MESH)
        return 0

    def greet_box(j, _):
        pl.semaphore_signal(barrier, inc=1, device_id={"box": lax.rem(g + j, nbox)}, device_id_type=MESH)
        return 0

    lax.fori_loop(1, nslab, greet_slab, 0)
    lax.fori_loop(1, nbox, greet_box, 0)

    def weigh(i, _):
        lower = wl[i].astype(F32) * (1.0 / WDEN)
        upper = wu[i].astype(F32) * (1.0 / WDEN)
        own_c = jnp.where(bl[i] == g, lower, 0.0) + jnp.where(bu[i] == g, upper, 0.0)
        below_c = jnp.where(bl[i] == g - 1, lower, 0.0)
        above_c = jnp.where(bu[i] == g + 1, upper, 0.0)
        plane = cone[i].reshape(nslab, rows, ny)
        z_up[:, i] = (above_c * plane).astype(z_up.dtype)
        z_dn[:, i] = (below_c * plane).astype(z_dn.dtype)
        own[:, i] = own_c * plane
        return 0

    lax.fori_loop(0, depth, weigh, 0)
    pl.semaphore_wait(barrier, nslab - 1 + nbox - 1)

    def up_copy(t):
        return pltpu.make_async_remote_copy(
            src_ref=z_up.at[t],
            dst_ref=from_below.at[t],
            send_sem=up_s.at[t],
            recv_sem=up_r.at[t],
            device_id={"box": lax.rem(g + 1, nbox)},
            device_id_type=MESH,
        )

    def dn_copy(t):
        return pltpu.make_async_remote_copy(
            src_ref=z_dn.at[t],
            dst_ref=from_above.at[t],
            send_sem=dn_s.at[t],
            recv_sem=dn_r.at[t],
            device_id={"box": lax.rem(g + nbox - 1, nbox)},
            device_id_type=MESH,
        )

    def send_z(j, _):
        t = lax.rem(me + 1 + j, nslab)

        @pl.when(g < nbox - 1)
        def _():
            up_copy(t).start()

        @pl.when(g > 0)
        def _():
            dn_copy(t).start()

        return 0

    lax.fori_loop(0, nslab, send_z, 0)

    h_copy.wait()

    def turn(c, _):
        for z in range(depth):
            ht[pl.ds(pl.multiple_of(c * ny, ny), ny), z * nx : (z + 1) * nx] = hbuf[c, z].T
        return 0

    lax.fori_loop(0, ch, turn, 0)

    def merge(t):
        @pl.when(g < nbox - 1)
        def _():
            dn_copy(t).wait_recv()
            own[t] = own[t] + from_above[t].astype(F32)

        @pl.when(g > 0)
        def _():
            up_copy(t).wait_recv()
            own[t] = own[t] + from_below[t].astype(F32)

    def a_copy(t, source):
        return pltpu.make_async_remote_copy(
            src_ref=send_a.at[t],
            dst_ref=recv_a.at[pl.ds(source * depth, depth)],
            send_sem=a_s.at[t],
            recv_sem=a_r.at[source],
            device_id={"slab": t},
            device_id_type=MESH,
        )

    def merge_send(j, _):
        t = lax.rem(me + 1 + j, nslab)
        merge(t)
        send_a[t] = own[t].astype(BF16)
        a_copy(t, me).start()
        return 0

    lax.fori_loop(0, nslab - 1, merge_send, 0)
    merge(me)
    recv_a[pl.ds(me * depth, depth)] = own[me].astype(BF16)

    y_in = lax.broadcasted_iota(jnp.int32, (ny, ny), 0)
    y_out = lax.broadcasted_iota(jnp.int32, (ny, ny), 1)
    hits = [y_in == lax.rem(y_out - dy + ny, ny) for dy in (-1, 0, 1)]
    taps = weight[...].astype(F32)
    for k in range(27):
        wide[k] = jnp.broadcast_to(taps[:, k : k + 1], (ch, ny))

    def fill(p, _):
        for cc in range(2):
            for j in range(9):
                block = jnp.zeros((ny, ny), F32)
                for d in range(3):
                    block = jnp.where(hits[d], wide[3 * j + d, pl.ds(2 * p + cc, 1)], block)
                wmat[p, j * ny : (j + 1) * ny, cc * ny : (cc + 1) * ny] = block.astype(BF16)
        return 0

    lax.fori_loop(0, pairs, fill, 0)

    def wait_a(j, _):
        source = lax.rem(me + j, nslab)
        a_copy(source, source).wait_recv()
        return 0

    lax.fori_loop(1, nslab, wait_a, 0)

    offset = jnp.where(bl[0] == g, plo[0], pup[0]) - me * depth

    def wanted(s, q):
        return recv_a[lax.rem(s * depth - 1 + q - offset + 2 * nz, nz)]

    def b_copy(s, source):
        return pltpu.make_async_remote_copy(
            src_ref=send_b.at[s],
            dst_ref=recv_b.at[source],
            send_sem=b_s.at[s],
            recv_sem=b_r.at[source],
            device_id={"slab": s},
            device_id_type=MESH,
        )

    def turn_send(j, _):
        s = lax.rem(me + 1 + j, nslab)
        for q in range(depth + 2):
            send_b[s, q] = wanted(s, q)
        b_copy(s, me).start()
        return 0

    lax.fori_loop(0, nslab - 1, turn_send, 0)
    for q in range(depth + 2):
        recv_b[me, q] = wanted(me, q)

    def wait_b(j, _):
        source = lax.rem(me + j, nslab)
        b_copy(source, source).wait_recv()
        return 0

    lax.fori_loop(1, nslab, wait_b, 0)

    for q in range(depth + 2):
        plane = recv_b[:, q].astype(F32).reshape(nx, ny)
        for dx in (-1, 0, 1):
            moved = (plane if dx == 0 else pltpu.roll(plane, dx % nx, 0)).astype(BF16)
            for dz in (-1, 0, 1):
                z, j = q + dz - 1, (dz + 1) * 3 + dx + 1
                if 0 <= z < depth:
                    lmat[z * nx : (z + 1) * nx, j * ny : (j + 1) * ny] = moved

    part[...] = jnp.zeros_like(part)
    picks = [y_out == lax.rem(y_in - dy + ny, ny) for dy in (-1, 0, 1)]

    def pair_terms(p, _):
        prod = jnp.dot(
            ht[pl.ds(pl.multiple_of(p * 2 * ny, 2 * ny), 2 * ny), :], lmat[...], preferred_element_type=F32
        )
        for cc in range(2):
            for j in range(9):
                block = prod[cc * ny : (cc + 1) * ny, j * ny : (j + 1) * ny]
                for d in range(3):
                    row = cc * TAP_ROWS + 3 * j + d
                    part[p, row : row + 1] = jnp.sum(jnp.where(picks[d], block, 0.0), axis=0, keepdims=True)
        return 0

    lax.fori_loop(0, pairs, pair_terms, 0)
    msg[...] = jnp.zeros_like(msg)
    for half in range(pairs // 2):
        both = part[2 * half : 2 * half + 2].reshape(4 * TAP_ROWS, ny)
        msg[half : half + 1] = jnp.sum(both.T, axis=0, keepdims=True)

    def c_copy(s, source):
        return pltpu.make_async_remote_copy(
            src_ref=msg,
            dst_ref=slab_terms.at[source],
            send_sem=c_s.at[s],
            recv_sem=c_r.at[source],
            device_id={"slab": s},
            device_id_type=MESH,
        )

    def d_copy(b, source):
        return pltpu.make_async_remote_copy(
            src_ref=msg2,
            dst_ref=box_terms.at[source],
            send_sem=d_s.at[b],
            recv_sem=d_r.at[source],
            device_id={"box": b},
            device_id_type=MESH,
        )

    def send_c(j, _):
        c_copy(lax.rem(me + j, nslab), me).start()
        return 0

    def send_d(j, _):
        d_copy(lax.rem(g + j, nbox), g).start()
        return 0

    def wait_c(j, _):
        source = lax.rem(me + j, nslab)
        c_copy(source, source).wait_recv()
        return 0

    def wait_d(j, _):
        source = lax.rem(g + j, nbox)
        d_copy(source, source).wait_recv()
        return 0

    def o_copy(p):
        return pltpu.make_async_copy(obuf.at[pl.ds(2 * p, 2)], out_hbm.at[pl.ds(2 * p, 2)], osem.at[p])

    def pair_grads(p, _):
        grads = jnp.dot(lmat[...], wmat[p], preferred_element_type=F32)
        for cc in range(2):
            obuf[2 * p + cc] = grads[:, cc * ny : (cc + 1) * ny].reshape(depth, nx, ny).astype(BF16)
        o_copy(p).start()
        return 0

    slab_terms[me] = msg[...]
    lax.fori_loop(1, nslab, send_c, 0)
    lax.fori_loop(0, pairs // 2, pair_grads, 0)
    lax.fori_loop(1, nslab, wait_c, 0)
    total = slab_terms[0]
    for s in range(1, nslab):
        total = total + slab_terms[s]
    msg2[...] = total
    box_terms[g] = total
    lax.fori_loop(1, nbox, send_d, 0)
    lax.fori_loop(pairs // 2, pairs, pair_grads, 0)
    lax.fori_loop(1, nbox, wait_d, 0)
    total = box_terms[0]
    for b in range(1, nbox):
        total = total + box_terms[b]
    total = total * scale
    for c in range(ch):
        at = (c % 4) * TAP_ROWS
        wg[c : c + 1, :] = total[c // 4 : c // 4 + 1, at : at + 27]

    def drain_z(t, _):
        @pl.when(g < nbox - 1)
        def _():
            up_copy(t).wait_send()

        @pl.when(g > 0)
        def _():
            dn_copy(t).wait_send()

        return 0

    def drain_slab(j, _):
        s = lax.rem(me + j, nslab)
        a_copy(s, me).wait_send()
        b_copy(s, me).wait_send()
        c_copy(s, me).wait_send()
        return 0

    def drain_box(j, _):
        d_copy(lax.rem(g + j, nbox), g).wait_send()
        return 0

    def drain_out(p, _):
        o_copy(p).wait()
        return 0

    lax.fori_loop(0, nslab, drain_z, 0)
    lax.fori_loop(1, nslab, drain_slab, 0)
    lax.fori_loop(1, nbox, drain_box, 0)
    lax.fori_loop(0, pairs, drain_out, 0)


def local(
    nbox,
    nslab,
    hidden_field,
    cone_grad,
    conv_weight,
    box_lower,
    box_upper,
    plane_lower,
    plane_upper,
    weight_lower,
    weight_upper,
):
    _, ch, depth, nx, ny = hidden_field.shape
    rows = nx // nslab
    nz = depth * nslab
    scale = 1.0 / math.sqrt(nbox * nz * nx * ny)
    vmem = pl.BlockSpec(memory_space=pltpu.VMEM)
    smem = pl.BlockSpec(memory_space=pltpu.SMEM)
    anywhere = pl.BlockSpec(memory_space=pl.ANY)
    dma = pltpu.SemaphoreType.DMA
    link = BF16
    hidden_grad, weight_grad = pl.pallas_call(
        functools.partial(kernel, nbox, nslab, scale),
        out_shape=(
            jax.ShapeDtypeStruct((ch, depth, nx, ny), BF16),
            jax.ShapeDtypeStruct((ch, 27), F32),
        ),
        in_specs=[smem] * 6 + [vmem, vmem, anywhere],
        out_specs=(anywhere, vmem),
        scratch_shapes=[
            pltpu.VMEM((ch, depth, nx, ny), BF16),
            pltpu.VMEM((nslab, depth, rows, ny), F32),
            pltpu.VMEM((nslab, depth, rows, ny), link),
            pltpu.VMEM((nslab, depth, rows, ny), link),
            pltpu.VMEM((nslab, depth, rows, ny), link),
            pltpu.VMEM((nslab, depth, rows, ny), link),
            pltpu.VMEM((nslab, depth, rows, ny), BF16),
            pltpu.VMEM((nz, rows, ny), BF16),
            pltpu.VMEM((nslab, depth + 2, rows, ny), BF16),
            pltpu.VMEM((nslab, depth + 2, rows, ny), BF16),
            pltpu.VMEM((ch * ny, depth * nx), BF16),
            pltpu.VMEM((ch // 2, 9 * ny, 2 * ny), BF16),
            pltpu.VMEM((27, ch, ny), F32),
            pltpu.VMEM((depth * nx, 9 * ny), BF16),
            pltpu.VMEM((ch // 2, 2 * TAP_ROWS, ny), F32),
            pltpu.VMEM((ch, depth, nx, ny), BF16),
            pltpu.VMEM((8, 128), F32),
            pltpu.VMEM((nslab, 8, 128), F32),
            pltpu.VMEM((8, 128), F32),
            pltpu.VMEM((nbox, 8, 128), F32),
            dma,
            dma((nslab,)),
            dma((nslab,)),
            dma((nslab,)),
            dma((nslab,)),
            dma((nslab,)),
            dma((nslab,)),
            dma((nslab,)),
            dma((nslab,)),
            dma((nslab,)),
            dma((nslab,)),
            dma((nbox,)),
            dma((nbox,)),
            dma((ch // 2,)),
        ],
        compiler_params=pltpu.CompilerParams(
            collective_id=0, has_side_effects=True, vmem_limit_bytes=44 * 2**20
        ),
    )(
        box_lower,
        box_upper,
        plane_lower,
        plane_upper,
        weight_lower,
        weight_upper,
        cone_grad,
        conv_weight,
        hidden_field.reshape(ch, depth, nx, ny),
    )
    return hidden_grad.reshape(hidden_field.shape), weight_grad


def solution(mesh):
    in_specs = (
        P("box", None, "slab", None, None),
        P(("box", "slab"), None, None),
        P(),
        P(("box", "slab")),
        P(("box", "slab")),
        P(("box", "slab")),
        P(("box", "slab")),
        P(("box", "slab")),
        P(("box", "slab")),
    )
    out_specs = (P("box", None, "slab", None, None), P())
    return jax.shard_map(
        functools.partial(local, mesh.shape["box"], mesh.shape["slab"]),
        mesh=mesh,
        in_specs=in_specs,
        out_specs=out_specs,
        check_vma=False,
    )
```

```python
import functools
import math

import jax
import jax.numpy as jnp
from jax import lax
from jax.experimental import pallas as pl
from jax.experimental.pallas import tpu as pltpu
from jax.sharding import PartitionSpec as P

WDEN = 256
MESH = pl.DeviceIdType.MESH
F32 = jnp.float32
BF16 = jnp.bfloat16
TAP_ROWS = 32


def kernel(
    nbox,
    nslab,
    scale,
    bl_hbm,
    bu_hbm,
    plo_hbm,
    pup_hbm,
    wl_hbm,
    wu_hbm,
    cone_hbm,
    weight_hbm,
    h_hbm,
    out_hbm,
    wg,
    bl,
    bu,
    plo,
    pup,
    wl,
    wu,
    cone,
    weight,
    hbuf,
    own,
    z_up,
    z_dn,
    from_above,
    from_below,
    send_a,
    recv_a,
    send_b,
    recv_b,
    ht,
    wmat,
    wide,
    lmat,
    part,
    obuf,
    msg,
    slab_terms,
    msg2,
    box_terms,
    isem,
    hsem,
    up_s,
    up_r,
    dn_s,
    dn_r,
    a_s,
    a_r,
    b_s,
    b_r,
    c_s,
    c_r,
    d_s,
    d_r,
    osem,
):
    g = lax.axis_index("box")
    me = lax.axis_index("slab")
    depth, nx, ny = cone.shape
    rows = nx // nslab
    nz = depth * nslab
    ch = hbuf.shape[0]
    pairs = ch // 2

    loads = [
        pltpu.make_async_copy(source, held, isem.at[i])
        for i, (source, held) in enumerate(
            (
                (cone_hbm, cone),
                (bl_hbm, bl),
                (bu_hbm, bu),
                (wl_hbm, wl),
                (wu_hbm, wu),
                (plo_hbm, plo),
                (pup_hbm, pup),
                (weight_hbm, weight),
            )
        )
    ]
    for load in loads:
        load.start()
    h_copy = pltpu.make_async_copy(h_hbm, hbuf, hsem)
    h_copy.start()

    barrier = pltpu.get_barrier_semaphore()

    def greet_slab(j, _):
        pl.semaphore_signal(barrier, inc=1, device_id={"slab": lax.rem(me + j, nslab)}, device_id_type=MESH)
        return 0

    def greet_box(j, _):
        pl.semaphore_signal(barrier, inc=1, device_id={"box": lax.rem(g + j, nbox)}, device_id_type=MESH)
        return 0

    lax.fori_loop(1, nslab, greet_slab, 0)
    lax.fori_loop(1, nbox, greet_box, 0)

    for load in loads:
        load.wait()

    def weigh(i, _):
        lower = wl[i].astype(F32) * (1.0 / WDEN)
        upper = wu[i].astype(F32) * (1.0 / WDEN)
        own_c = jnp.where(bl[i] == g, lower, 0.0) + jnp.where(bu[i] == g, upper, 0.0)
        below_c = jnp.where(bl[i] == g - 1, lower, 0.0)
        above_c = jnp.where(bu[i] == g + 1, upper, 0.0)
        plane = cone[i].reshape(nslab, rows, ny)
        z_up[:, i] = (above_c * plane).astype(z_up.dtype)
        z_dn[:, i] = (below_c * plane).astype(z_dn.dtype)
        own[:, i] = own_c * plane
        return 0

    lax.fori_loop(0, depth, weigh, 0)
    pl.semaphore_wait(barrier, nslab - 1 + nbox - 1)

    def up_copy(t):
        return pltpu.make_async_remote_copy(
            src_ref=z_up.at[t],
            dst_ref=from_below.at[t],
            send_sem=up_s.at[t],
            recv_sem=up_r.at[t],
            device_id={"box": lax.rem(g + 1, nbox)},
            device_id_type=MESH,
        )

    def dn_copy(t):
        return pltpu.make_async_remote_copy(
            src_ref=z_dn.at[t],
            dst_ref=from_above.at[t],
            send_sem=dn_s.at[t],
            recv_sem=dn_r.at[t],
            device_id={"box": lax.rem(g + nbox - 1, nbox)},
            device_id_type=MESH,
        )

    def send_z(j, _):
        t = lax.rem(me + 1 + j, nslab)

        @pl.when(g < nbox - 1)
        def _():
            up_copy(t).start()

        @pl.when(g > 0)
        def _():
            dn_copy(t).start()

        return 0

    lax.fori_loop(0, nslab, send_z, 0)

    h_copy.wait()

    def turn(c, _):
        for z in range(depth):
            ht[pl.ds(pl.multiple_of(c * ny, ny), ny), z * nx : (z + 1) * nx] = hbuf[c, z].T
        return 0

    lax.fori_loop(0, ch, turn, 0)

    def merge(t):
        @pl.when(g < nbox - 1)
        def _():
            dn_copy(t).wait_recv()
            own[t] = own[t] + from_above[t].astype(F32)

        @pl.when(g > 0)
        def _():
            up_copy(t).wait_recv()
            own[t] = own[t] + from_below[t].astype(F32)

    def a_copy(t, source):
        return pltpu.make_async_remote_copy(
            src_ref=send_a.at[t],
            dst_ref=recv_a.at[pl.ds(source * depth, depth)],
            send_sem=a_s.at[t],
            recv_sem=a_r.at[source],
            device_id={"slab": t},
            device_id_type=MESH,
        )

    def merge_send(j, _):
        t = lax.rem(me + 1 + j, nslab)
        merge(t)
        send_a[t] = own[t].astype(BF16)
        a_copy(t, me).start()
        return 0

    lax.fori_loop(0, nslab - 1, merge_send, 0)
    merge(me)
    recv_a[pl.ds(me * depth, depth)] = own[me].astype(BF16)

    y_in = lax.broadcasted_iota(jnp.int32, (ny, ny), 0)
    y_out = lax.broadcasted_iota(jnp.int32, (ny, ny), 1)
    hits = [y_in == lax.rem(y_out - dy + ny, ny) for dy in (-1, 0, 1)]
    taps = weight[...].astype(F32)
    for k in range(27):
        wide[k] = jnp.broadcast_to(taps[:, k : k + 1], (ch, ny))

    def fill(p, _):
        for cc in range(2):
            for j in range(9):
                block = jnp.zeros((ny, ny), F32)
                for d in range(3):
                    block = jnp.where(hits[d], wide[3 * j + d, pl.ds(2 * p + cc, 1)], block)
                wmat[p, j * ny : (j + 1) * ny, cc * ny : (cc + 1) * ny] = block.astype(BF16)
        return 0

    lax.fori_loop(0, pairs, fill, 0)

    def wait_a(j, _):
        source = lax.rem(me + j, nslab)
        a_copy(source, source).wait_recv()
        return 0

    lax.fori_loop(1, nslab, wait_a, 0)

    offset = jnp.where(bl[0] == g, plo[0], pup[0]) - me * depth

    def wanted(s, q):
        return recv_a[lax.rem(s * depth - 1 + q - offset + 2 * nz, nz)]

    def b_copy(s, source):
        return pltpu.make_async_remote_copy(
            src_ref=send_b.at[s],
            dst_ref=recv_b.at[source],
            send_sem=b_s.at[s],
            recv_sem=b_r.at[source],
            device_id={"slab": s},
            device_id_type=MESH,
        )

    def turn_send(j, _):
        s = lax.rem(me + 1 + j, nslab)
        for q in range(depth + 2):
            send_b[s, q] = wanted(s, q)
        b_copy(s, me).start()
        return 0

    lax.fori_loop(0, nslab - 1, turn_send, 0)
    for q in range(depth + 2):
        recv_b[me, q] = wanted(me, q)

    def wait_b(j, _):
        source = lax.rem(me + j, nslab)
        b_copy(source, source).wait_recv()
        return 0

    lax.fori_loop(1, nslab, wait_b, 0)

    for q in range(depth + 2):
        plane = recv_b[:, q].astype(F32).reshape(nx, ny)
        for dx in (-1, 0, 1):
            moved = (plane if dx == 0 else pltpu.roll(plane, dx % nx, 0)).astype(BF16)
            for dz in (-1, 0, 1):
                z, j = q + dz - 1, (dz + 1) * 3 + dx + 1
                if 0 <= z < depth:
                    lmat[z * nx : (z + 1) * nx, j * ny : (j + 1) * ny] = moved

    part[...] = jnp.zeros_like(part)
    picks = [y_out == lax.rem(y_in - dy + ny, ny) for dy in (-1, 0, 1)]

    def pair_terms(p, _):
        prod = jnp.dot(
            ht[pl.ds(pl.multiple_of(p * 2 * ny, 2 * ny), 2 * ny), :], lmat[...], preferred_element_type=F32
        )
        for cc in range(2):
            for j in range(9):
                block = prod[cc * ny : (cc + 1) * ny, j * ny : (j + 1) * ny]
                for d in range(3):
                    row = cc * TAP_ROWS + 3 * j + d
                    part[p, row : row + 1] = jnp.sum(jnp.where(picks[d], block, 0.0), axis=0, keepdims=True)
        return 0

    lax.fori_loop(0, pairs, pair_terms, 0)
    msg[...] = jnp.zeros_like(msg)
    for half in range(pairs // 2):
        both = part[2 * half : 2 * half + 2].reshape(4 * TAP_ROWS, ny)
        msg[half : half + 1] = jnp.sum(both.T, axis=0, keepdims=True)

    def c_copy(s, source):
        return pltpu.make_async_remote_copy(
            src_ref=msg,
            dst_ref=slab_terms.at[source],
            send_sem=c_s.at[s],
            recv_sem=c_r.at[source],
            device_id={"slab": s},
            device_id_type=MESH,
        )

    def d_copy(b, source):
        return pltpu.make_async_remote_copy(
            src_ref=msg2,
            dst_ref=box_terms.at[source],
            send_sem=d_s.at[b],
            recv_sem=d_r.at[source],
            device_id={"box": b},
            device_id_type=MESH,
        )

    def send_c(j, _):
        c_copy(lax.rem(me + j, nslab), me).start()
        return 0

    def send_d(j, _):
        d_copy(lax.rem(g + j, nbox), g).start()
        return 0

    def wait_c(j, _):
        source = lax.rem(me + j, nslab)
        c_copy(source, source).wait_recv()
        return 0

    def wait_d(j, _):
        source = lax.rem(g + j, nbox)
        d_copy(source, source).wait_recv()
        return 0

    def o_copy(p):
        return pltpu.make_async_copy(obuf.at[pl.ds(2 * p, 2)], out_hbm.at[pl.ds(2 * p, 2)], osem.at[p])

    def pair_grads(p, _):
        grads = jnp.dot(lmat[...], wmat[p], preferred_element_type=F32)
        for cc in range(2):
            obuf[2 * p + cc] = grads[:, cc * ny : (cc + 1) * ny].reshape(depth, nx, ny).astype(BF16)
        o_copy(p).start()
        return 0

    slab_terms[me] = msg[...]
    lax.fori_loop(1, nslab, send_c, 0)
    lax.fori_loop(0, pairs // 2, pair_grads, 0)
    lax.fori_loop(1, nslab, wait_c, 0)
    total = slab_terms[0]
    for s in range(1, nslab):
        total = total + slab_terms[s]
    msg2[...] = total
    box_terms[g] = total
    lax.fori_loop(1, nbox, send_d, 0)
    lax.fori_loop(pairs // 2, pairs, pair_grads, 0)
    lax.fori_loop(1, nbox, wait_d, 0)
    total = box_terms[0]
    for b in range(1, nbox):
        total = total + box_terms[b]
    total = total * scale
    for c in range(ch):
        at = (c % 4) * TAP_ROWS
        wg[c : c + 1, :] = total[c // 4 : c // 4 + 1, at : at + 27]

    def drain_z(t, _):
        @pl.when(g < nbox - 1)
        def _():
            up_copy(t).wait_send()

        @pl.when(g > 0)
        def _():
            dn_copy(t).wait_send()

        return 0

    def drain_slab(j, _):
        s = lax.rem(me + j, nslab)
        a_copy(s, me).wait_send()
        b_copy(s, me).wait_send()
        c_copy(s, me).wait_send()
        return 0

    def drain_box(j, _):
        d_copy(lax.rem(g + j, nbox), g).wait_send()
        return 0

    def drain_out(p, _):
        o_copy(p).wait()
        return 0

    lax.fori_loop(0, nslab, drain_z, 0)
    lax.fori_loop(1, nslab, drain_slab, 0)
    lax.fori_loop(1, nbox, drain_box, 0)
    lax.fori_loop(0, pairs, drain_out, 0)


def local(
    nbox,
    nslab,
    hidden_field,
    cone_grad,
    conv_weight,
    box_lower,
    box_upper,
    plane_lower,
    plane_upper,
    weight_lower,
    weight_upper,
):
    _, ch, depth, nx, ny = hidden_field.shape
    rows = nx // nslab
    nz = depth * nslab
    scale = 1.0 / math.sqrt(nbox * nz * nx * ny)
    vmem = pl.BlockSpec(memory_space=pltpu.VMEM)
    hbm = pl.BlockSpec(memory_space=pltpu.HBM)
    anywhere = pl.BlockSpec(memory_space=pl.ANY)
    dma = pltpu.SemaphoreType.DMA
    link = BF16
    hidden_grad, weight_grad = pl.pallas_call(
        functools.partial(kernel, nbox, nslab, scale),
        out_shape=(
            jax.ShapeDtypeStruct((ch, depth, nx, ny), BF16),
            jax.ShapeDtypeStruct((ch, 27), F32),
        ),
        in_specs=[hbm] * 9,
        out_specs=(anywhere, vmem),
        scratch_shapes=[
            *[pltpu.SMEM((depth,), jnp.int32)] * 6,
            pltpu.VMEM(cone_grad.shape, F32),
            pltpu.VMEM(conv_weight.shape, BF16),
            pltpu.VMEM((ch, depth, nx, ny), BF16),
            pltpu.VMEM((nslab, depth, rows, ny), F32),
            pltpu.VMEM((nslab, depth, rows, ny), link),
            pltpu.VMEM((nslab, depth, rows, ny), link),
            pltpu.VMEM((nslab, depth, rows, ny), link),
            pltpu.VMEM((nslab, depth, rows, ny), link),
            pltpu.VMEM((nslab, depth, rows, ny), BF16),
            pltpu.VMEM((nz, rows, ny), BF16),
            pltpu.VMEM((nslab, depth + 2, rows, ny), BF16),
            pltpu.VMEM((nslab, depth + 2, rows, ny), BF16),
            pltpu.VMEM((ch * ny, depth * nx), BF16),
            pltpu.VMEM((ch // 2, 9 * ny, 2 * ny), BF16),
            pltpu.VMEM((27, ch, ny), F32),
            pltpu.VMEM((depth * nx, 9 * ny), BF16),
            pltpu.VMEM((ch // 2, 2 * TAP_ROWS, ny), F32),
            pltpu.VMEM((ch, depth, nx, ny), BF16),
            pltpu.VMEM((8, 128), F32),
            pltpu.VMEM((nslab, 8, 128), F32),
            pltpu.VMEM((8, 128), F32),
            pltpu.VMEM((nbox, 8, 128), F32),
            dma((8,)),
            dma,
            dma((nslab,)),
            dma((nslab,)),
            dma((nslab,)),
            dma((nslab,)),
            dma((nslab,)),
            dma((nslab,)),
            dma((nslab,)),
            dma((nslab,)),
            dma((nslab,)),
            dma((nslab,)),
            dma((nbox,)),
            dma((nbox,)),
            dma((ch // 2,)),
        ],
        compiler_params=pltpu.CompilerParams(
            collective_id=0, has_side_effects=True, vmem_limit_bytes=int(62 * 2**20)
        ),
    )(
        box_lower,
        box_upper,
        plane_lower,
        plane_upper,
        weight_lower,
        weight_upper,
        cone_grad,
        conv_weight,
        hidden_field.reshape(ch, depth, nx, ny),
    )
    return hidden_grad.reshape(hidden_field.shape), weight_grad


def solution(mesh):
    in_specs = (
        P("box", None, "slab", None, None),
        P(("box", "slab"), None, None),
        P(),
        P(("box", "slab")),
        P(("box", "slab")),
        P(("box", "slab")),
        P(("box", "slab")),
        P(("box", "slab")),
        P(("box", "slab")),
    )
    out_specs = (P("box", None, "slab", None, None), P())
    return jax.shard_map(
        functools.partial(local, mesh.shape["box"], mesh.shape["slab"]),
        mesh=mesh,
        in_specs=in_specs,
        out_specs=out_specs,
        check_vma=False,
    )
```

```python
import functools
import math

import jax
import jax.numpy as jnp
from jax import lax
from jax.experimental import pallas as pl
from jax.experimental.pallas import tpu as pltpu
from jax.sharding import PartitionSpec as P

WDEN = 256
MESH = pl.DeviceIdType.MESH
F32 = jnp.float32
BF16 = jnp.bfloat16
TAP_ROWS = 32


def kernel(
    nbox,
    nslab,
    scale,
    bl_hbm,
    bu_hbm,
    plo_hbm,
    pup_hbm,
    wl_hbm,
    wu_hbm,
    cone_hbm,
    weight_hbm,
    h_hbm,
    out,
    wg,
    bl,
    bu,
    plo,
    pup,
    wl,
    wu,
    cone,
    weight,
    hbuf,
    own,
    z_up,
    z_dn,
    from_above,
    from_below,
    send_a,
    recv_a,
    send_b,
    recv_b,
    ht,
    wmat,
    wide,
    lmat,
    part,
    msg,
    slab_terms,
    msg2,
    box_terms,
    isem,
    hsem,
    up_s,
    up_r,
    dn_s,
    dn_r,
    a_s,
    a_r,
    b_s,
    b_r,
    c_s,
    c_r,
    d_s,
    d_r,
):
    g = lax.axis_index("box")
    me = lax.axis_index("slab")
    depth, nx, ny = cone.shape
    rows = nx // nslab
    nz = depth * nslab
    ch = hbuf.shape[0]
    pairs = ch // 2

    loads = [
        pltpu.make_async_copy(source, held, isem.at[i])
        for i, (source, held) in enumerate(
            (
                (cone_hbm, cone),
                (bl_hbm, bl),
                (bu_hbm, bu),
                (wl_hbm, wl),
                (wu_hbm, wu),
                (plo_hbm, plo),
                (pup_hbm, pup),
                (weight_hbm, weight),
            )
        )
    ]
    for load in loads:
        load.start()
    h_copy = pltpu.make_async_copy(h_hbm, hbuf, hsem)
    h_copy.start()

    barrier = pltpu.get_barrier_semaphore()

    def greet_slab(j, _):
        pl.semaphore_signal(barrier, inc=1, device_id={"slab": lax.rem(me + j, nslab)}, device_id_type=MESH)
        return 0

    def greet_box(j, _):
        pl.semaphore_signal(barrier, inc=1, device_id={"box": lax.rem(g + j, nbox)}, device_id_type=MESH)
        return 0

    lax.fori_loop(1, nslab, greet_slab, 0)
    lax.fori_loop(1, nbox, greet_box, 0)

    for load in loads:
        load.wait()

    def weigh(i, _):
        lower = wl[i].astype(F32) * (1.0 / WDEN)
        upper = wu[i].astype(F32) * (1.0 / WDEN)
        own_c = jnp.where(bl[i] == g, lower, 0.0) + jnp.where(bu[i] == g, upper, 0.0)
        below_c = jnp.where(bl[i] == g - 1, lower, 0.0)
        above_c = jnp.where(bu[i] == g + 1, upper, 0.0)
        plane = cone[i].reshape(nslab, rows, ny)
        z_up[:, i] = (above_c * plane).astype(z_up.dtype)
        z_dn[:, i] = (below_c * plane).astype(z_dn.dtype)
        own[:, i] = own_c * plane
        return 0

    lax.fori_loop(0, depth, weigh, 0)
    pl.semaphore_wait(barrier, nslab - 1 + nbox - 1)

    def up_copy(t):
        return pltpu.make_async_remote_copy(
            src_ref=z_up.at[t],
            dst_ref=from_below.at[t],
            send_sem=up_s.at[t],
            recv_sem=up_r.at[t],
            device_id={"box": lax.rem(g + 1, nbox)},
            device_id_type=MESH,
        )

    def dn_copy(t):
        return pltpu.make_async_remote_copy(
            src_ref=z_dn.at[t],
            dst_ref=from_above.at[t],
            send_sem=dn_s.at[t],
            recv_sem=dn_r.at[t],
            device_id={"box": lax.rem(g + nbox - 1, nbox)},
            device_id_type=MESH,
        )

    def send_z(j, _):
        t = lax.rem(me + 1 + j, nslab)

        @pl.when(g < nbox - 1)
        def _():
            up_copy(t).start()

        @pl.when(g > 0)
        def _():
            dn_copy(t).start()

        return 0

    lax.fori_loop(0, nslab, send_z, 0)

    h_copy.wait()

    def turn(c, _):
        for z in range(depth):
            ht[pl.ds(pl.multiple_of(c * ny, ny), ny), z * nx : (z + 1) * nx] = hbuf[c, z].T
        return 0

    lax.fori_loop(0, ch, turn, 0)

    def merge(t):
        @pl.when(g < nbox - 1)
        def _():
            dn_copy(t).wait_recv()
            own[t] = own[t] + from_above[t].astype(F32)

        @pl.when(g > 0)
        def _():
            up_copy(t).wait_recv()
            own[t] = own[t] + from_below[t].astype(F32)

    def a_copy(t, source):
        return pltpu.make_async_remote_copy(
            src_ref=send_a.at[t],
            dst_ref=recv_a.at[pl.ds(source * depth, depth)],
            send_sem=a_s.at[t],
            recv_sem=a_r.at[source],
            device_id={"slab": t},
            device_id_type=MESH,
        )

    def merge_send(j, _):
        t = lax.rem(me + 1 + j, nslab)
        merge(t)
        send_a[t] = own[t].astype(BF16)
        a_copy(t, me).start()
        return 0

    lax.fori_loop(0, nslab - 1, merge_send, 0)
    merge(me)
    recv_a[pl.ds(me * depth, depth)] = own[me].astype(BF16)

    y_in = lax.broadcasted_iota(jnp.int32, (ny, ny), 0)
    y_out = lax.broadcasted_iota(jnp.int32, (ny, ny), 1)
    hits = [y_in == lax.rem(y_out - dy + ny, ny) for dy in (-1, 0, 1)]
    taps = weight[...].astype(F32)
    for k in range(27):
        wide[k] = jnp.broadcast_to(taps[:, k : k + 1], (ch, ny))

    def fill(p, _):
        for cc in range(2):
            for j in range(9):
                block = jnp.zeros((ny, ny), F32)
                for d in range(3):
                    block = jnp.where(hits[d], wide[3 * j + d, pl.ds(2 * p + cc, 1)], block)
                wmat[p, j * ny : (j + 1) * ny, cc * ny : (cc + 1) * ny] = block.astype(BF16)
        return 0

    lax.fori_loop(0, pairs, fill, 0)

    def wait_a(j, _):
        source = lax.rem(me + j, nslab)
        a_copy(source, source).wait_recv()
        return 0

    lax.fori_loop(1, nslab, wait_a, 0)

    offset = jnp.where(bl[0] == g, plo[0], pup[0]) - me * depth

    def wanted(s, q):
        return recv_a[lax.rem(s * depth - 1 + q - offset + 2 * nz, nz)]

    def b_copy(s, source):
        return pltpu.make_async_remote_copy(
            src_ref=send_b.at[s],
            dst_ref=recv_b.at[source],
            send_sem=b_s.at[s],
            recv_sem=b_r.at[source],
            device_id={"slab": s},
            device_id_type=MESH,
        )

    def turn_send(j, _):
        s = lax.rem(me + 1 + j, nslab)
        for q in range(depth + 2):
            send_b[s, q] = wanted(s, q)
        b_copy(s, me).start()
        return 0

    lax.fori_loop(0, nslab - 1, turn_send, 0)
    for q in range(depth + 2):
        recv_b[me, q] = wanted(me, q)

    def wait_b(j, _):
        source = lax.rem(me + j, nslab)
        b_copy(source, source).wait_recv()
        return 0

    lax.fori_loop(1, nslab, wait_b, 0)

    for q in range(depth + 2):
        plane = recv_b[:, q].astype(F32).reshape(nx, ny)
        for dx in (-1, 0, 1):
            moved = (plane if dx == 0 else pltpu.roll(plane, dx % nx, 0)).astype(BF16)
            for dz in (-1, 0, 1):
                z, j = q + dz - 1, (dz + 1) * 3 + dx + 1
                if 0 <= z < depth:
                    lmat[z * nx : (z + 1) * nx, j * ny : (j + 1) * ny] = moved

    part[...] = jnp.zeros_like(part)
    picks = [y_out == lax.rem(y_in - dy + ny, ny) for dy in (-1, 0, 1)]

    def pair_terms(p, _):
        prod = jnp.dot(
            ht[pl.ds(pl.multiple_of(p * 2 * ny, 2 * ny), 2 * ny), :], lmat[...], preferred_element_type=F32
        )
        for cc in range(2):
            for j in range(9):
                block = prod[cc * ny : (cc + 1) * ny, j * ny : (j + 1) * ny]
                for d in range(3):
                    row = cc * TAP_ROWS + 3 * j + d
                    part[p, row : row + 1] = jnp.sum(jnp.where(picks[d], block, 0.0), axis=0, keepdims=True)
        return 0

    lax.fori_loop(0, pairs, pair_terms, 0)
    msg[...] = jnp.zeros_like(msg)
    for half in range(pairs // 2):
        both = part[2 * half : 2 * half + 2].reshape(4 * TAP_ROWS, ny)
        msg[half : half + 1] = jnp.sum(both.T, axis=0, keepdims=True)

    def c_copy(s, source):
        return pltpu.make_async_remote_copy(
            src_ref=msg,
            dst_ref=slab_terms.at[source],
            send_sem=c_s.at[s],
            recv_sem=c_r.at[source],
            device_id={"slab": s},
            device_id_type=MESH,
        )

    def d_copy(b, source):
        return pltpu.make_async_remote_copy(
            src_ref=msg2,
            dst_ref=box_terms.at[source],
            send_sem=d_s.at[b],
            recv_sem=d_r.at[source],
            device_id={"box": b},
            device_id_type=MESH,
        )

    def send_c(j, _):
        c_copy(lax.rem(me + j, nslab), me).start()
        return 0

    def send_d(j, _):
        d_copy(lax.rem(g + j, nbox), g).start()
        return 0

    def wait_c(j, _):
        source = lax.rem(me + j, nslab)
        c_copy(source, source).wait_recv()
        return 0

    def wait_d(j, _):
        source = lax.rem(g + j, nbox)
        d_copy(source, source).wait_recv()
        return 0

    def pair_grads(p, _):
        grads = jnp.dot(lmat[...], wmat[p], preferred_element_type=F32)
        for cc in range(2):
            out[2 * p + cc] = grads[:, cc * ny : (cc + 1) * ny].reshape(depth, nx, ny).astype(BF16)
        return 0

    slab_terms[me] = msg[...]
    lax.fori_loop(1, nslab, send_c, 0)
    lax.fori_loop(0, pairs // 2, pair_grads, 0)
    lax.fori_loop(1, nslab, wait_c, 0)
    total = slab_terms[0]
    for s in range(1, nslab):
        total = total + slab_terms[s]
    msg2[...] = total
    box_terms[g] = total
    lax.fori_loop(1, nbox, send_d, 0)
    lax.fori_loop(pairs // 2, pairs, pair_grads, 0)
    lax.fori_loop(1, nbox, wait_d, 0)
    total = box_terms[0]
    for b in range(1, nbox):
        total = total + box_terms[b]
    total = total * scale
    for c in range(ch):
        at = (c % 4) * TAP_ROWS
        wg[c : c + 1, :] = total[c // 4 : c // 4 + 1, at : at + 27]

    def drain_z(t, _):
        @pl.when(g < nbox - 1)
        def _():
            up_copy(t).wait_send()

        @pl.when(g > 0)
        def _():
            dn_copy(t).wait_send()

        return 0

    def drain_slab(j, _):
        s = lax.rem(me + j, nslab)
        a_copy(s, me).wait_send()
        b_copy(s, me).wait_send()
        c_copy(s, me).wait_send()
        return 0

    def drain_box(j, _):
        d_copy(lax.rem(g + j, nbox), g).wait_send()
        return 0

    lax.fori_loop(0, nslab, drain_z, 0)
    lax.fori_loop(1, nslab, drain_slab, 0)
    lax.fori_loop(1, nbox, drain_box, 0)


def local(
    nbox,
    nslab,
    hidden_field,
    cone_grad,
    conv_weight,
    box_lower,
    box_upper,
    plane_lower,
    plane_upper,
    weight_lower,
    weight_upper,
):
    _, ch, depth, nx, ny = hidden_field.shape
    rows = nx // nslab
    nz = depth * nslab
    scale = 1.0 / math.sqrt(nbox * nz * nx * ny)
    vmem = pl.BlockSpec(memory_space=pltpu.VMEM)
    hbm = pl.BlockSpec(memory_space=pltpu.HBM)
    dma = pltpu.SemaphoreType.DMA
    link = BF16
    hidden_grad, weight_grad = pl.pallas_call(
        functools.partial(kernel, nbox, nslab, scale),
        out_shape=(
            pltpu.VMEM((ch, depth, nx, ny), BF16),
            jax.ShapeDtypeStruct((ch, 27), F32),
        ),
        in_specs=[hbm] * 9,
        out_specs=(vmem, vmem),
        scratch_shapes=[
            *[pltpu.SMEM((depth,), jnp.int32)] * 6,
            pltpu.VMEM(cone_grad.shape, F32),
            pltpu.VMEM(conv_weight.shape, BF16),
            pltpu.VMEM((ch, depth, nx, ny), BF16),
            pltpu.VMEM((nslab, depth, rows, ny), F32),
            pltpu.VMEM((nslab, depth, rows, ny), link),
            pltpu.VMEM((nslab, depth, rows, ny), link),
            pltpu.VMEM((nslab, depth, rows, ny), link),
            pltpu.VMEM((nslab, depth, rows, ny), link),
            pltpu.VMEM((nslab, depth, rows, ny), BF16),
            pltpu.VMEM((nz, rows, ny), BF16),
            pltpu.VMEM((nslab, depth + 2, rows, ny), BF16),
            pltpu.VMEM((nslab, depth + 2, rows, ny), BF16),
            pltpu.VMEM((ch * ny, depth * nx), BF16),
            pltpu.VMEM((ch // 2, 9 * ny, 2 * ny), BF16),
            pltpu.VMEM((27, ch, ny), F32),
            pltpu.VMEM((depth * nx, 9 * ny), BF16),
            pltpu.VMEM((ch // 2, 2 * TAP_ROWS, ny), F32),
            pltpu.VMEM((8, 128), F32),
            pltpu.VMEM((nslab, 8, 128), F32),
            pltpu.VMEM((8, 128), F32),
            pltpu.VMEM((nbox, 8, 128), F32),
            dma((8,)),
            dma,
            dma((nslab,)),
            dma((nslab,)),
            dma((nslab,)),
            dma((nslab,)),
            dma((nslab,)),
            dma((nslab,)),
            dma((nslab,)),
            dma((nslab,)),
            dma((nslab,)),
            dma((nslab,)),
            dma((nbox,)),
            dma((nbox,)),
        ],
        compiler_params=pltpu.CompilerParams(
            collective_id=0, has_side_effects=True, vmem_limit_bytes=int(44 * 2**20)
        ),
    )(
        *(
            pltpu.with_memory_space_constraint(x, pltpu.HBM)
            for x in (
                box_lower,
                box_upper,
                plane_lower,
                plane_upper,
                weight_lower,
                weight_upper,
                cone_grad,
                conv_weight,
                hidden_field.reshape(ch, depth, nx, ny),
            )
        )
    )
    return hidden_grad.reshape(hidden_field.shape), weight_grad


def solution(mesh):
    in_specs = (
        P("box", None, "slab", None, None),
        P(("box", "slab"), None, None),
        P(),
        P(("box", "slab")),
        P(("box", "slab")),
        P(("box", "slab")),
        P(("box", "slab")),
        P(("box", "slab")),
        P(("box", "slab")),
    )
    out_specs = (P("box", None, "slab", None, None), P())
    return jax.shard_map(
        functools.partial(local, mesh.shape["box"], mesh.shape["slab"]),
        mesh=mesh,
        in_specs=in_specs,
        out_specs=out_specs,
        check_vma=False,
    )
```
